32 devices in a mesh: groups: 2 (over x), ep: 16 (over z, y, core).
Axes of the slice: x: 2, y: 2, z: 4, core: 2. Of those that a mesh axis runs over, the one named last changes fastest.
Arguments:
- inputs: float32 [64, 6144], P(('groups', 'ep')), parts along dimension 0, may hold values from -6 to 6
- norm_gain: float32 [6144], replicated, may hold values from 0.5 to 1.5
- dense_gate: bfloat16 [6144, 12288], P(None, 'ep'), may hold values from -0.078125 to 0.078125
- dense_up: bfloat16 [6144, 12288], P(None, 'ep'), may hold values from -0.078125 to 0.078125
- dense_down: bfloat16 [12288, 6144], P('ep'), may hold values from -0.0546875 to 0.0546875
- expert_gate: bfloat16 [6144, 32768], P(None, 'ep'), may hold values from -0.078125 to 0.078125
- expert_up: bfloat16 [6144, 32768], P(None, 'ep'), may hold values from -0.078125 to 0.078125
- expert_down: bfloat16 [32768, 6144], P('ep'), may hold values from -0.125 to 0.125
- expert_ids: int32 [64, 12], P('groups'), parts along dimension 0, may hold values from 0 to 16, all different within a row; in each aligned block of 2 rows (0 to 1, 2 to 3, ...) at most 2 rows name the same one
- route_weights: int32 [64, 12], P('groups'), parts along dimension 0, may hold values from 1 to 1024
- out_gain: float32 [6144], replicated, may hold values from 0.5 to 1.5
Outputs:
- result: float32 [64, 6144], P(('groups', 'ep')), parts along dimension 0
The draws below stay inside these ranges and needn't reach their ends.
There are 2 independent parts, one for each index of `groups`. The reference program is written for one: setup_inputs(seed, part) draws one part's arguments, and reference() takes and returns one part's arrays. A program takes and returns all parts, laid end to end along the dimension named above; an argument that names none is the same for every part. Nothing has to cross between parts.
Inputs may be any that keep to these rules, and one draw needn't show every extreme that they name: `expert_ids`: each row names 12 different values; in the rows of one device (aligned blocks of 2 rows) no value is named by more than 2 rows, and in every draw some value is named by exactly 2 rows of one device.
All inputs are finite; a program needn't handle non-finite values.
Results may differ from the reference program's by a relative error of at most 0.0031.
Values may be sent and summed in bfloat16 or wider, within the bound.
No kernel may reach another device: no remote copies, remote signals or barrier semaphores. Data moves between devices by JAX's collectives and lax.ppermute only.
A program may use at most 192 MiB of HBM per device.

```python
import math
import jax
import jax.numpy as jnp
import numpy as np
from jax import lax

D = 6144
FF = 12288
EF = 2048
EXPERTS = 16
TOPK = 12
ROWS_DEV = 2
MOST = 2
TOKENS = 32
N_EP = 16


def with_ends(array, rng, smallest, high):
    extent = array.shape
    spot = [jax.random.randint(jax.random.fold_in(rng, axis), (), 0, extent[axis]) for axis in range(len(extent))]
    array = array.at[tuple(spot)].set(smallest)
    longest = extent.index(max(extent))
    spot[longest] = (spot[longest] + 1) % extent[longest]
    return array.at[tuple(spot)].set(high)


def steps_of(rng, extent, pieces, low, largest):
    level, own = 1.0, jax.random.fold_in(rng, 6)
    for dim, blocks in pieces:
        steps = jnp.exp(jax.random.uniform(jax.random.fold_in(own, dim), (blocks,), jnp.float32, low / len(pieces), largest / len(pieces)))
        level = level * jnp.repeat(steps, extent[dim] // blocks).reshape([-1 if axis == dim else 1 for axis in range(len(extent))])
    return level


def shared_out(key, own, number, rows, number_of, top, reach, slope):
    sequence = jax.random.permutation(key, number_of)
    crowded, ordinary = portions_of(number_of, rows * top, reach, slope, True), portions_of(number_of, rows * top, reach, slope, False)
    places = jnp.arange(number_of)

    def named(lengths, turn):
        used = int((lengths > 0).sum())
        fixed = max(1, used // 4)
        moved = fixed + (places - fixed + turn * (used - fixed)) % max(1, number_of - fixed)
        return jnp.zeros((number_of,), jnp.int32).at[sequence[jnp.where(places < fixed, places, moved)]].set(jnp.asarray(lengths, jnp.int32))

    lengths = jnp.where(number % 4 == 0, named(crowded, number // 4), named(ordinary, number - number // 4 - 1))
    mixed = jax.random.permutation(jax.random.fold_in(own, 3), number_of)
    source_of, taker = mixed[0:number_of // 2 * 2:2], mixed[1:number_of // 2 * 2:2]
    slack = jnp.minimum(lengths[source_of] - 1, reach - lengths[taker]) // 2
    slack = jnp.where((source_of == sequence[0]) | (taker == sequence[0]) | (lengths[taker] == 0), 0, jnp.maximum(slack, 0))
    moved = jax.random.randint(jax.random.fold_in(own, 4), (number_of // 2,), 0, 1 << 20) % (slack + 1)
    lengths = lengths.at[source_of].add(-moved).at[taker].add(moved)
    members = jnp.searchsorted(jnp.cumsum(lengths), jnp.arange(rows * top), side="right").astype(jnp.int32)
    table = members.reshape(top, rows).T
    table = table[jax.random.permutation(jax.random.fold_in(own, 1), rows)]
    turn = jax.random.randint(jax.random.fold_in(own, 2), (rows, 1), 0, top)
    return jnp.take_along_axis(table, (jnp.arange(top)[None, :] + turn) % top, axis=1)


def portions_of(count, total, limit, slope, full):
    portions = [(1 << 20) // math.isqrt(standing ** slope) + 1 for standing in range(1, count + 1)]
    largest = limit if full else min(limit, max(-(-total // count), total * portions[0] // sum(portions)))
    least = 1 if total - largest >= count - 1 else 0
    counts, rest = [largest] + [least] * (count - 1), total - largest - least * (count - 1)
    while rest > 0:
        free = [i for i in range(1, count) if counts[i] < largest] or [i for i in range(1, count) if counts[i] < limit]
        mass, left = sum([portions[i] for i in free]), rest
        for i in free:
            more = min(limit - counts[i], max(1, left * portions[i] // mass), rest)
            counts[i] = counts[i] + more
            rest = rest - more
    return np.array(counts)


def bell_draw(key, extent, scale, reach, split=(), kind=jnp.bfloat16):
    drawn = jax.random.normal(key, extent, jnp.float32) * scale
    if len(split) > 0:
        drawn = steps_of(key, extent, split, -0.22, 0.18) * drawn
    return jnp.clip(drawn, min=-reach, max=reach).astype(kind)


def setup_inputs(seed: int = 0, part: int = 0) -> dict:
    splits = jax.random.split(jax.random.key(seed), 12)
    part_splits = jax.random.split(jax.random.fold_in(splits[11], part), 12)
    inputs = bell_draw(part_splits[0], (TOKENS, D), 1.0, 6.0, ((0, 16),), jnp.float32)
    norm_gain = jnp.clip(1.0 + 0.1 * jax.random.normal(splits[1], (D,), jnp.float32), 0.5, 1.5)
    dense_gate = bell_draw(splits[2], (D, FF), D ** -0.5, 0.078125, ((1, 16),))
    dense_up = bell_draw(splits[3], (D, FF), D ** -0.5, 0.078125, ((1, 16),))
    dense_down = bell_draw(splits[4], (FF, D), FF ** -0.5, 0.0546875, ((0, 16),))
    expert_gate = bell_draw(splits[5], (D, EXPERTS * EF), D ** -0.5, 0.078125, ((1, 16),))
    expert_up = bell_draw(splits[6], (D, EXPERTS * EF), D ** -0.5, 0.078125, ((1, 16),))
    expert_down = bell_draw(splits[7], (EXPERTS * EF, D), EF ** -0.5, 0.125, ((0, 16),))
    expert_ids_keys = jax.random.split(jax.random.fold_in(part_splits[8], 1), TOKENS // ROWS_DEV)
    expert_ids_turns = jax.random.permutation(jax.random.fold_in(part_splits[8], 3), TOKENS // ROWS_DEV)
    expert_ids = jax.vmap(lambda own, number: shared_out(jax.random.fold_in(part_splits[8], 2), own, number, ROWS_DEV, EXPERTS + 1, TOPK, MOST, 1))(expert_ids_keys, expert_ids_turns).reshape((TOKENS, TOPK))
    route_weights = with_ends(jax.random.randint(part_splits[9], (TOKENS, TOPK), 1, 1025), jax.random.fold_in(part_splits[9], 1), 1, 1024).astype(jnp.int32)
    out_gain = jnp.clip(1.0 + 0.1 * jax.random.normal(splits[10], (D,), jnp.float32), 0.5, 1.5)
    return dict(inputs=inputs, norm_gain=norm_gain, dense_gate=dense_gate, dense_up=dense_up, dense_down=dense_down, expert_gate=expert_gate, expert_up=expert_up, expert_down=expert_down, expert_ids=expert_ids, route_weights=route_weights, out_gain=out_gain)


def rms_scale(values):
    return values * lax.rsqrt(lax.optimization_barrier(jnp.mean(values * values, axis=-1, keepdims=True)) + 1e-06)

def slot_table(expert_ids, weights_all, expert, blocks, block_rows):
    matches = expert_ids == expert
    picked = jnp.any(matches, axis=1).reshape(blocks, block_rows)
    weight = lax.optimization_barrier(jnp.sum(jnp.where(matches, weights_all, 0.0), axis=1)).reshape(blocks, block_rows)
    ranking = jnp.cumsum(picked.astype(jnp.int32), axis=1) - 1
    position = lax.broadcasted_iota(jnp.int32, (blocks, block_rows), 1)
    row_cols = []
    weight_cols = []
    for column in range(MOST):
        chosen = picked & (ranking == column)
        row_cols.append(lax.optimization_barrier(jnp.sum(jnp.where(chosen, position, 0), axis=1)).astype(jnp.int32))
        weight_cols.append(lax.optimization_barrier(jnp.sum(jnp.where(chosen, weight, 0.0), axis=1)))
    offsets = (lax.broadcasted_iota(jnp.int32, (blocks, 1), 0) * block_rows).astype(jnp.int32)
    slot_rows = (jnp.stack(row_cols, axis=1) + offsets).reshape(-1).astype(jnp.int32)
    slot_weight = jnp.stack(weight_cols, axis=1).reshape(-1)
    return (slot_rows, slot_weight)

def reference(inputs, norm_gain, dense_gate, dense_up, dense_down, expert_gate, expert_up, expert_down, expert_ids, route_weights, out_gain):
    hidden_in = (rms_scale(inputs) * norm_gain).astype(jnp.bfloat16)
    gate = jnp.dot(hidden_in, dense_gate, preferred_element_type=jnp.float32)
    upper = jnp.dot(hidden_in, dense_up, preferred_element_type=jnp.float32)
    dense_hidden = (jax.nn.silu(gate) * upper).astype(jnp.bfloat16)
    dense = jnp.dot(dense_hidden, dense_down, preferred_element_type=jnp.float32)
    weights_all = route_weights.astype(jnp.float32) / 1024.0
    zero_weight = lax.optimization_barrier(jnp.sum(jnp.where(expert_ids == EXPERTS, weights_all, 0.0), axis=1))
    start_moe = zero_weight[:, None] * hidden_in.astype(jnp.float32)

    def add_expert(expert, moe):
        slot_rows, slot_weight = slot_table(expert_ids, weights_all, expert, N_EP, ROWS_DEV)
        picked_in = hidden_in[slot_rows]
        column = (expert * EF).astype(jnp.int32)
        w_gate = lax.dynamic_slice_in_dim(expert_gate, column, EF, 1)
        w_upper = lax.dynamic_slice_in_dim(expert_up, column, EF, 1)
        w_down = lax.dynamic_slice_in_dim(expert_down, column, EF, 0)
        e_gate = jnp.dot(picked_in, w_gate, preferred_element_type=jnp.float32)
        e_upper = jnp.dot(picked_in, w_upper, preferred_element_type=jnp.float32)
        e_hidden = (jax.nn.silu(e_gate) * e_upper).astype(jnp.bfloat16)
        outcome = jnp.dot(e_hidden, w_down, preferred_element_type=jnp.float32) * slot_weight[:, None]
        return moe.at[slot_rows].add(outcome)
    moe = lax.fori_loop(0, EXPERTS, add_expert, start_moe)
    joined = dense + moe
    return inputs + rms_scale(joined) * out_gain
```

```python
import functools

import jax
import jax.numpy as jnp
from jax import lax
from jax.experimental import pallas as pl
from jax.experimental.pallas import tpu as pltpu
from jax.sharding import PartitionSpec as P

EXPERTS = 16
BF16, F32 = jnp.bfloat16, jnp.float32
VMEM = pl.BlockSpec(memory_space=pltpu.VMEM)
SMEM = pl.BlockSpec(memory_space=pltpu.SMEM)
HBM = pl.BlockSpec(memory_space=pl.ANY)


def in_hbm(array):
    return pltpu.with_memory_space_constraint(array, pltpu.HBM)


def in_vmem(array):
    return pltpu.with_memory_space_constraint(array, pltpu.VMEM)


def block_of(extent, most):
    fits = [b for b in range(128, min(most, extent) + 1, 128) if extent % b == 0]
    return fits[-1] if fits else extent


def rms_scale(values):
    return values * lax.rsqrt(jnp.mean(values * values, axis=-1, keepdims=True) + 1e-06)


def norm_rows(inputs_ref, gain_ref, out_ref):
    out_ref[...] = (rms_scale(inputs_ref[...]) * gain_ref[...]).astype(out_ref.dtype)


def normed(inputs, gain):
    return pl.pallas_call(
        norm_rows,
        out_shape=jax.ShapeDtypeStruct(inputs.shape, BF16),
        in_specs=[VMEM, VMEM],
        out_specs=VMEM,
        compiler_params=pltpu.CompilerParams(vmem_limit_bytes=8 << 20),
    )(inputs, gain.reshape(1, -1))


class Stream:
    def __init__(self, sources, slots, sems, steps, at):
        self.sources, self.slots, self.sems, self.steps, self.at = sources, slots, sems, steps, at
        self.depth = slots[0].shape[0]

    def copies(self, step, slot):
        return [
            pltpu.make_async_copy(self.at(source, step), buffer.at[slot], self.sems.at[i, slot])
            for i, (source, buffer) in enumerate(zip(self.sources, self.slots))
        ]

    def fill(self):
        for step in range(min(self.depth, self.steps)):
            for copy in self.copies(step, step):
                copy.start()

    def run(self, use):
        def body(step, _):
            slot = lax.rem(step, self.depth)
            for copy in self.copies(step, slot):
                copy.wait()
            use(step, [buffer.at[slot] for buffer in self.slots])

            @pl.when(step + self.depth < self.steps)
            def _():
                for copy in self.copies(step + self.depth, slot):
                    copy.start()

            return 0

        lax.fori_loop(0, self.steps, body, 0)


def aligned(step, size):
    return pl.ds(pl.multiple_of(step * size, size), size)


def column_weights(expert, ids_ref, route_ref):
    count = ids_ref.shape[1]
    across = jnp.sum(
        jnp.where(ids_ref[...] == expert, route_ref[...].astype(F32) / 1024.0, 0.0),
        axis=0,
        keepdims=True,
    )
    same = lax.broadcasted_iota(jnp.int32, (count, count), 0) == lax.broadcasted_iota(
        jnp.int32, (count, count), 1
    )
    return jnp.sum(jnp.where(same, across, 0.0), axis=1, keepdims=True)


def branches(
    expert_ref,
    rows_ref,
    ids_ref,
    route_ref,
    eg_ref,
    eu_ref,
    dg_ref,
    du_ref,
    dd_ref,
    ed_ref,
    out_ref,
    eg_slots,
    eu_slots,
    dg_slots,
    du_slots,
    dd_slots,
    ed_slots,
    eg_sum,
    eu_sum,
    dg_sum,
    du_sum,
    first_sems,
    second_sems,
):
    width = rows_ref.shape[1]
    kb, cb = eg_slots.shape[1], dd_slots.shape[2]
    first = Stream(
        [eg_ref, eu_ref, dg_ref, du_ref],
        [eg_slots, eu_slots, dg_slots, du_slots],
        first_sems,
        width // kb,
        lambda ref, step: ref.at[aligned(step, kb), :],
    )
    second = Stream(
        [dd_ref, ed_ref],
        [dd_slots, ed_slots],
        second_sems,
        width // cb,
        lambda ref, step: ref.at[:, aligned(step, cb)],
    )
    first.fill()
    second.fill()
    sums = [eg_sum, eu_sum, dg_sum, du_sum]
    for total in sums:
        total[...] = jnp.zeros_like(total)

    def gate_up(step, blocks):
        part = rows_ref[:, aligned(step, kb)]
        for total, block in zip(sums, blocks):
            total[...] += jnp.dot(part, block[...], preferred_element_type=F32)

    first.run(gate_up)
    e_hidden = (jax.nn.silu(eg_sum[...]) * eu_sum[...]).astype(BF16)
    d_hidden = (jax.nn.silu(dg_sum[...]) * du_sum[...]).astype(BF16)
    weight = column_weights(expert_ref[0], ids_ref, route_ref)

    def down(step, blocks):
        dense = jnp.dot(d_hidden, blocks[0][...], preferred_element_type=F32)
        routed = jnp.dot(e_hidden, blocks[1][...], preferred_element_type=F32)
        out_ref[:, aligned(step, cb)] = (dense + routed * weight).astype(out_ref.dtype)

    second.run(down)


def branch_sums(expert, rows, ids, route, e_gate, e_up, d_gate, d_up, d_down, e_down):
    count, width = rows.shape
    dense, units = d_gate.shape[1], e_gate.shape[1]
    kb, cb = block_of(width, 256), block_of(width, 512)
    depth = 3
    weights = [in_hbm(a) for a in (e_gate, e_up, d_gate, d_up, d_down, e_down)]
    return pl.pallas_call(
        branches,
        out_shape=jax.ShapeDtypeStruct((count, width), BF16),
        in_specs=[SMEM, VMEM, VMEM, VMEM] + [HBM] * 6,
        out_specs=VMEM,
        scratch_shapes=[
            pltpu.VMEM((depth, kb, units), BF16),
            pltpu.VMEM((depth, kb, units), BF16),
            pltpu.VMEM((depth, kb, dense), BF16),
            pltpu.VMEM((depth, kb, dense), BF16),
            pltpu.VMEM((depth, dense, cb), BF16),
            pltpu.VMEM((depth, units, cb), BF16),
            pltpu.VMEM((count, units), F32),
            pltpu.VMEM((count, units), F32),
            pltpu.VMEM((count, dense), F32),
            pltpu.VMEM((count, dense), F32),
            pltpu.SemaphoreType.DMA((4, depth)),
            pltpu.SemaphoreType.DMA((2, depth)),
        ],
        compiler_params=pltpu.CompilerParams(vmem_limit_bytes=40 << 20),
        cost_estimate=pl.CostEstimate(
            flops=6 * count * width * (dense + units),
            bytes_accessed=6 * width * (dense + units),
            transcendentals=count * (dense + units),
        ),
    )(expert, rows, ids, route, *weights)


def join(
    first_ref, received_ref, hidden_ref, ids_ref, route_ref, inputs_ref, gain_ref, out_ref
):
    rows = inputs_ref.shape[0]
    summed = jnp.sum(received_ref[...].astype(F32), axis=0)
    count = ids_ref.shape[1]
    across = jnp.sum(
        jnp.where(ids_ref[...] == EXPERTS, route_ref[...].astype(F32) / 1024.0, 0.0),
        axis=0,
        keepdims=True,
    )
    mine = lax.broadcasted_iota(jnp.int32, (rows, count), 1) == first_ref[
        0
    ] + lax.broadcasted_iota(jnp.int32, (rows, count), 0)
    zero_weight = jnp.sum(jnp.where(mine, across, 0.0), axis=1, keepdims=True)
    joined = summed + zero_weight * hidden_ref[...].astype(F32)
    out_ref[...] = inputs_ref[...] + rms_scale(joined) * gain_ref[...]


def joined_rows(first, received, hidden, ids, route, inputs, gain):
    return pl.pallas_call(
        join,
        out_shape=jax.ShapeDtypeStruct(inputs.shape, F32),
        in_specs=[SMEM] + [VMEM] * 6,
        out_specs=VMEM,
        compiler_params=pltpu.CompilerParams(vmem_limit_bytes=24 << 20),
    )(first, in_vmem(received), hidden, ids, route, inputs, gain.reshape(1, -1))


def on_device(
    inputs,
    norm_gain,
    dense_gate,
    dense_up,
    dense_down,
    expert_gate,
    expert_up,
    expert_down,
    expert_ids,
    route_weights,
    out_gain,
):
    devices = lax.axis_size("ep")
    rows_own, width = inputs.shape
    my_index = lax.axis_index("ep")
    expert = my_index // (devices // EXPERTS)
    ids, route = expert_ids.T, route_weights.T
    hidden_in = normed(inputs, norm_gain)
    gathered = lax.all_gather(hidden_in, "ep", axis=0, tiled=True)
    partial = branch_sums(
        expert[None],
        gathered,
        ids,
        route,
        expert_gate,
        expert_up,
        dense_gate,
        dense_up,
        dense_down,
        expert_down,
    )
    received = lax.all_to_all(
        partial.reshape(devices, rows_own, width), "ep", 0, 0, tiled=True
    )
    return joined_rows(
        (my_index * rows_own)[None], received, hidden_in, ids, route, inputs, out_gain
    )


def solution(mesh):
    placed = (
        P(("groups", "ep"), None),
        P(),
        P(None, "ep"),
        P(None, "ep"),
        P("ep", None),
        P(None, "ep"),
        P(None, "ep"),
        P("ep", None),
        P("groups", None),
        P("groups", None),
        P(),
    )
    return jax.shard_map(
        on_device, mesh=mesh, in_specs=placed, out_specs=P(("groups", "ep"), None), check_vma=False
    )
```

```python
import functools

import jax
import jax.numpy as jnp
from jax import lax
from jax.experimental import pallas as pl
from jax.experimental.pallas import tpu as pltpu
from jax.sharding import PartitionSpec as P

EXPERTS = 16
FLOPS_PER_BYTE = 1000
BF16, F32 = jnp.bfloat16, jnp.float32
VMEM = pl.BlockSpec(memory_space=pltpu.VMEM)
SMEM = pl.BlockSpec(memory_space=pltpu.SMEM)
HBM = pl.BlockSpec(memory_space=pl.ANY)


def in_hbm(array):
    return pltpu.with_memory_space_constraint(array, pltpu.HBM)


def in_vmem(array):
    return pltpu.with_memory_space_constraint(array, pltpu.VMEM)


def block_of(extent, most):
    fits = [b for b in range(128, min(most, extent) + 1, 128) if extent % b == 0]
    return fits[-1] if fits else extent


def rms_scale(values):
    return values * lax.rsqrt(jnp.mean(values * values, axis=-1, keepdims=True) + 1e-06)


def norm_rows(inputs_ref, gain_ref, out_ref):
    out_ref[...] = (rms_scale(inputs_ref[...]) * gain_ref[...]).astype(out_ref.dtype)


def normed(inputs, gain, ahead):
    return pl.pallas_call(
        norm_rows,
        out_shape=jax.ShapeDtypeStruct(inputs.shape, BF16),
        in_specs=[VMEM, VMEM],
        out_specs=VMEM,
        compiler_params=pltpu.CompilerParams(vmem_limit_bytes=1 << 20),
        cost_estimate=pl.CostEstimate(
            flops=FLOPS_PER_BYTE * ahead, bytes_accessed=inputs.nbytes, transcendentals=0
        ),
    )(inputs, gain.reshape(1, -1))


class Stream:
    def __init__(self, sources, slots, sems, steps, at):
        self.sources, self.slots, self.sems, self.steps, self.at = sources, slots, sems, steps, at
        self.depth = slots[0].shape[0]

    def copies(self, step, slot):
        return [
            pltpu.make_async_copy(self.at(source, step), buffer.at[slot], self.sems.at[i, slot])
            for i, (source, buffer) in enumerate(zip(self.sources, self.slots))
        ]

    def fill(self):
        for step in range(min(self.depth, self.steps)):
            for copy in self.copies(step, step):
                copy.start()

    def run(self, use):
        def body(step, _):
            slot = lax.rem(step, self.depth)
            for copy in self.copies(step, slot):
                copy.wait()
            use(step, [buffer.at[slot] for buffer in self.slots])

            @pl.when(step + self.depth < self.steps)
            def _():
                for copy in self.copies(step + self.depth, slot):
                    copy.start()

            return 0

        lax.fori_loop(0, self.steps, body, 0)


def aligned(step, size):
    return pl.ds(pl.multiple_of(step * size, size), size)


def column_weights(expert, ids_ref, route_ref):
    count = ids_ref.shape[1]
    across = jnp.sum(
        jnp.where(ids_ref[...] == expert, route_ref[...].astype(F32) / 1024.0, 0.0),
        axis=0,
        keepdims=True,
    )
    same = lax.broadcasted_iota(jnp.int32, (count, count), 0) == lax.broadcasted_iota(
        jnp.int32, (count, count), 1
    )
    return jnp.sum(jnp.where(same, across, 0.0), axis=1, keepdims=True)


def branches(
    expert_ref,
    rows_ref,
    ids_ref,
    route_ref,
    eg_ref,
    eu_ref,
    dg_ref,
    du_ref,
    dd_ref,
    ed_ref,
    out_ref,
    eu_slots,
    dg_slots,
    du_slots,
    dd_slots,
    eg_sum,
    eu_sum,
    dg_sum,
    du_sum,
    rows_flat,
    first_sems,
    second_sems,
):
    count, width = rows_flat.shape
    rows_flat[...] = rows_ref[...].reshape(count, width)
    kb, cb = eu_slots.shape[1], dd_slots.shape[2]
    first = Stream(
        [eu_ref, dg_ref, du_ref],
        [eu_slots, dg_slots, du_slots],
        first_sems,
        width // kb,
        lambda ref, step: ref.at[aligned(step, kb), :],
    )
    second = Stream(
        [dd_ref],
        [dd_slots],
        second_sems,
        width // cb,
        lambda ref, step: ref.at[:, aligned(step, cb)],
    )
    first.fill()
    second.fill()
    sums = [eg_sum, eu_sum, dg_sum, du_sum]
    for total in sums:
        total[...] = jnp.zeros_like(total)

    def gate_up(step, blocks):
        at = aligned(step, kb)
        part = rows_flat[:, at]
        for total, block in zip(sums, [eg_ref.at[at, :]] + blocks):
            total[...] += jnp.dot(part, block[...], preferred_element_type=F32)

    first.run(gate_up)
    e_hidden = (jax.nn.silu(eg_sum[...]) * eu_sum[...]).astype(BF16)
    d_hidden = (jax.nn.silu(dg_sum[...]) * du_sum[...]).astype(BF16)
    weight = column_weights(expert_ref[0], ids_ref, route_ref)

    def down(step, blocks):
        at = aligned(step, cb)
        dense = jnp.dot(d_hidden, blocks[0][...], preferred_element_type=F32)
        routed = jnp.dot(e_hidden, ed_ref[:, at], preferred_element_type=F32)
        out_ref[:, at] = (dense + routed * weight).astype(out_ref.dtype)

    second.run(down)


def branch_sums(expert, rows, ids, route, e_gate, e_up, d_gate, d_up, d_down, e_down):
    count, width = rows.shape[0] * rows.shape[1], rows.shape[2]
    dense, units = d_gate.shape[1], e_gate.shape[1]
    kb, cb = block_of(width, 256), block_of(width, 512)
    depth = 3
    weights = [
        in_vmem(e_gate),
        in_hbm(e_up),
        in_hbm(d_gate),
        in_hbm(d_up),
        in_hbm(d_down),
        in_vmem(e_down),
    ]
    return pl.pallas_call(
        branches,
        out_shape=jax.ShapeDtypeStruct((count, width), BF16),
        in_specs=[SMEM, VMEM, VMEM, VMEM, VMEM, HBM, HBM, HBM, HBM, VMEM],
        out_specs=VMEM,
        scratch_shapes=[
            pltpu.VMEM((depth, kb, units), BF16),
            pltpu.VMEM((depth, kb, dense), BF16),
            pltpu.VMEM((depth, kb, dense), BF16),
            pltpu.VMEM((depth, dense, cb), BF16),
            pltpu.VMEM((count, units), F32),
            pltpu.VMEM((count, units), F32),
            pltpu.VMEM((count, dense), F32),
            pltpu.VMEM((count, dense), F32),
            pltpu.VMEM((count, width), BF16),
            pltpu.SemaphoreType.DMA((3, depth)),
            pltpu.SemaphoreType.DMA((1, depth)),
        ],
        compiler_params=pltpu.CompilerParams(vmem_limit_bytes=11 << 20),
        cost_estimate=pl.CostEstimate(
            flops=6 * count * width * (dense + units),
            bytes_accessed=6 * width * (dense + units),
            transcendentals=count * (dense + units),
        ),
    )(expert, in_vmem(rows), ids, route, *weights)


def join(
    first_ref, received_ref, hidden_ref, ids_ref, route_ref, inputs_ref, gain_ref, out_ref
):
    rows = inputs_ref.shape[0]
    summed = jnp.sum(received_ref[...].astype(F32), axis=0)
    count = ids_ref.shape[1]
    across = jnp.sum(
        jnp.where(ids_ref[...] == EXPERTS, route_ref[...].astype(F32) / 1024.0, 0.0),
        axis=0,
        keepdims=True,
    )
    mine = lax.broadcasted_iota(jnp.int32, (rows, count), 1) == first_ref[
        0
    ] + lax.broadcasted_iota(jnp.int32, (rows, count), 0)
    zero_weight = jnp.sum(jnp.where(mine, across, 0.0), axis=1, keepdims=True)
    joined = summed + zero_weight * hidden_ref[...].astype(F32)
    out_ref[...] = inputs_ref[...] + rms_scale(joined) * gain_ref[...]


def joined_rows(first, received, hidden, ids, route, inputs, gain):
    return pl.pallas_call(
        join,
        out_shape=jax.ShapeDtypeStruct(inputs.shape, F32),
        in_specs=[SMEM] + [VMEM] * 6,
        out_specs=VMEM,
        compiler_params=pltpu.CompilerParams(vmem_limit_bytes=24 << 20),
    )(first, in_vmem(received), hidden, ids, route, inputs, gain.reshape(1, -1))


def on_device(
    inputs,
    norm_gain,
    dense_gate,
    dense_up,
    dense_down,
    expert_gate,
    expert_up,
    expert_down,
    expert_ids,
    route_weights,
    out_gain,
):
    devices = lax.axis_size("ep")
    rows_own, width = inputs.shape
    my_index = lax.axis_index("ep")
    expert = my_index // (devices // EXPERTS)
    ids, route = expert_ids.T, route_weights.T
    hidden_in = normed(inputs, norm_gain, expert_gate.nbytes + expert_down.nbytes)
    gathered = lax.all_gather(hidden_in, "ep", axis=0, tiled=False)
    partial = branch_sums(
        expert[None],
        gathered,
        ids,
        route,
        expert_gate,
        expert_up,
        dense_gate,
        dense_up,
        dense_down,
        expert_down,
    )
    received = lax.all_to_all(
        partial.reshape(devices, rows_own, width), "ep", 0, 0, tiled=True
    )
    return joined_rows(
        (my_index * rows_own)[None], received, hidden_in, ids, route, inputs, out_gain
    )


def solution(mesh):
    placed = (
        P(("groups", "ep"), None),
        P(),
        P(None, "ep"),
        P(None, "ep"),
        P("ep", None),
        P(None, "ep"),
        P(None, "ep"),
        P("ep", None),
        P("groups", None),
        P("groups", None),
        P(),
    )
    return jax.shard_map(
        on_device, mesh=mesh, in_specs=placed, out_specs=P(("groups", "ep"), None), check_vma=False
    )
```

```python
import functools

import jax
import jax.numpy as jnp
from jax import lax
from jax.experimental import pallas as pl
from jax.experimental.pallas import tpu as pltpu
from jax.sharding import PartitionSpec as P

EXPERTS = 16
FLOPS_PER_BYTE = 1000
BF16, F32 = jnp.bfloat16, jnp.float32
VMEM = pl.BlockSpec(memory_space=pltpu.VMEM)
SMEM = pl.BlockSpec(memory_space=pltpu.SMEM)
HBM = pl.BlockSpec(memory_space=pl.ANY)


def in_hbm(array):
    return pltpu.with_memory_space_constraint(array, pltpu.HBM)


def in_vmem(array):
    return pltpu.with_memory_space_constraint(array, pltpu.VMEM)


def block_of(extent, most):
    fits = [b for b in range(128, min(most, extent) + 1, 128) if extent % b == 0]
    return fits[-1] if fits else extent


def rms_scale(values):
    return values * lax.rsqrt(jnp.mean(values * values, axis=-1, keepdims=True) + 1e-06)


def norm_rows(inputs_ref, gain_ref, out_ref):
    out_ref[...] = (rms_scale(inputs_ref[...]) * gain_ref[...]).astype(out_ref.dtype)


def normed(inputs, gain, ahead):
    return pl.pallas_call(
        norm_rows,
        out_shape=jax.ShapeDtypeStruct(inputs.shape, BF16),
        in_specs=[VMEM, VMEM],
        out_specs=VMEM,
        compiler_params=pltpu.CompilerParams(vmem_limit_bytes=1 << 20),
        cost_estimate=pl.CostEstimate(
            flops=FLOPS_PER_BYTE * ahead, bytes_accessed=inputs.nbytes, transcendentals=0
        ),
    )(in_hbm(inputs), in_hbm(gain.reshape(1, -1)))


def gathered_rows(own, axis):
    devices = lax.axis_size(axis)
    assert devices & (devices - 1) == 0
    rows, places = own[None], [0]
    stages = [[1 << b] for b in range(2, devices.bit_length() - 1)] + [[1, 2]]
    for bits in stages:
        among = [0]
        for bit in bits:
            among = among + [k | bit for k in among]
        groups = [[i | k for k in among] for i in range(devices) if not i & among[-1]]
        rows = lax.all_gather(rows, axis, axis=0, tiled=True, axis_index_groups=groups)
        places = [p | k for k in among for p in places]
    return rows, places


class Stream:
    def __init__(self, sources, slots, sems, steps, at):
        self.sources, self.slots, self.sems, self.steps, self.at = sources, slots, sems, steps, at
        self.depth = slots[0].shape[0]

    def copies(self, step, slot):
        return [
            pltpu.make_async_copy(self.at(source, step), buffer.at[slot], self.sems.at[i, slot])
            for i, (source, buffer) in enumerate(zip(self.sources, self.slots))
        ]

    def fill(self):
        for step in range(min(self.depth, self.steps)):
            for copy in self.copies(step, step):
                copy.start()

    def run(self, use):
        def body(step, _):
            slot = lax.rem(step, self.depth)
            for copy in self.copies(step, slot):
                copy.wait()
            use(step, [buffer.at[slot] for buffer in self.slots])

            @pl.when(step + self.depth < self.steps)
            def _():
                for copy in self.copies(step + self.depth, slot):
                    copy.start()

            return 0

        lax.fori_loop(0, self.steps, body, 0)


def aligned(step, size):
    return pl.ds(pl.multiple_of(step * size, size), size)


def column_weights(expert, places, ids_ref, route_ref):
    count = ids_ref.shape[1]
    rows = count // len(places)
    across = jnp.sum(
        jnp.where(ids_ref[...] == expert, route_ref[...].astype(F32) / 1024.0, 0.0),
        axis=0,
        keepdims=True,
    )
    at = lax.broadcasted_iota(jnp.int32, (count, 1), 0)
    row = jnp.zeros_like(at)
    for k, place in enumerate(places):
        shift = (place - k) * rows
        row = jnp.where((at >= k * rows) & (at < (k + 1) * rows), at + shift, row)
    same = row == lax.broadcasted_iota(jnp.int32, (count, count), 1)
    return jnp.sum(jnp.where(same, across, 0.0), axis=1, keepdims=True)


def branches(
    places,
    slices,
    me_ref,
    rows_ref,
    ids_ref,
    route_ref,
    eg_ref,
    eu_ref,
    dg_ref,
    du_ref,
    dd_ref,
    ed_ref,
    out_ref,
    eu_slots,
    dg_slots,
    du_slots,
    dd_slots,
    eg_sum,
    eu_sum,
    dg_sum,
    du_sum,
    rows_flat,
    first_sems,
    second_sems,
):
    count, width = rows_flat.shape
    rows = count // len(places)
    kb, cb = eu_slots.shape[1], dd_slots.shape[2]
    first = Stream(
        [eu_ref, dg_ref, du_ref],
        [eu_slots, dg_slots, du_slots],
        first_sems,
        width // kb,
        lambda ref, step: ref.at[aligned(step, kb), :],
    )
    second = Stream(
        [dd_ref],
        [dd_slots],
        second_sems,
        width // cb,
        lambda ref, step: ref.at[:, aligned(step, cb)],
    )
    first.fill()
    second.fill()
    rows_flat[...] = rows_ref[...].reshape(count, width)
    sums = [eg_sum, eu_sum, dg_sum, du_sum]
    for total in sums:
        total[...] = jnp.zeros_like(total)

    def gate_up(step, blocks):
        at = aligned(step, kb)
        part = rows_flat[:, at]
        for total, block in zip(sums, [eg_ref.at[at, :]] + blocks):
            total[...] += jnp.dot(part, block[...], preferred_element_type=F32)

    first.run(gate_up)
    e_hidden = (jax.nn.silu(eg_sum[...]) * eu_sum[...]).astype(BF16)
    d_hidden = (jax.nn.silu(dg_sum[...]) * du_sum[...]).astype(BF16)
    weight = column_weights(me_ref[0] // slices, places, ids_ref, route_ref)

    def down(step, blocks):
        at = aligned(step, cb)
        dense = jnp.dot(d_hidden, blocks[0][...], preferred_element_type=F32)
        routed = jnp.dot(e_hidden, ed_ref[:, at], preferred_element_type=F32)
        part = (dense + routed * weight).astype(out_ref.dtype).reshape(len(places), rows, cb)
        for k, place in enumerate(places):
            out_ref[place, :, at] = part[k]

    second.run(down)


def branch_sums(me, gathered, places, ids, route, e_gate, e_up, d_gate, d_up, d_down, e_down):
    devices, rows, width = gathered.shape
    count = devices * rows
    dense, units = d_gate.shape[1], e_gate.shape[1]
    kb, cb = block_of(width, 512), block_of(width, 512)
    depth = 2
    weights = [
        in_vmem(e_gate),
        in_hbm(e_up),
        in_hbm(d_gate),
        in_hbm(d_up),
        in_hbm(d_down),
        in_vmem(e_down),
    ]
    return pl.pallas_call(
        functools.partial(branches, places, devices // EXPERTS),
        out_shape=jax.ShapeDtypeStruct((devices, rows, width), BF16),
        in_specs=[SMEM] + [VMEM] * 4 + [HBM] * 4 + [VMEM],
        out_specs=VMEM,
        scratch_shapes=[
            pltpu.VMEM((depth, kb, units), BF16),
            pltpu.VMEM((depth, kb, dense), BF16),
            pltpu.VMEM((depth, kb, dense), BF16),
            pltpu.VMEM((depth, dense, cb), BF16),
            pltpu.VMEM((count, units), F32),
            pltpu.VMEM((count, units), F32),
            pltpu.VMEM((count, dense), F32),
            pltpu.VMEM((count, dense), F32),
            pltpu.VMEM((count, width), BF16),
            pltpu.SemaphoreType.DMA((3, depth)),
            pltpu.SemaphoreType.DMA((1, depth)),
        ],
        compiler_params=pltpu.CompilerParams(vmem_limit_bytes=11 << 20),
        cost_estimate=pl.CostEstimate(
            flops=6 * count * width * (dense + units),
            bytes_accessed=6 * width * (dense + units),
            transcendentals=count * (dense + units),
        ),
    )(me, in_vmem(gathered), ids, route, *weights)


def join(
    first_ref, received_ref, hidden_ref, ids_ref, route_ref, inputs_ref, gain_ref, out_ref
):
    rows = inputs_ref.shape[0]
    summed = jnp.sum(received_ref[...].astype(F32), axis=0)
    count = ids_ref.shape[1]
    across = jnp.sum(
        jnp.where(ids_ref[...] == EXPERTS, route_ref[...].astype(F32) / 1024.0, 0.0),
        axis=0,
        keepdims=True,
    )
    mine = lax.broadcasted_iota(jnp.int32, (rows, count), 1) == first_ref[
        0
    ] + lax.broadcasted_iota(jnp.int32, (rows, count), 0)
    zero_weight = jnp.sum(jnp.where(mine, across, 0.0), axis=1, keepdims=True)
    joined = summed + zero_weight * hidden_ref[...].astype(F32)
    out_ref[...] = inputs_ref[...] + rms_scale(joined) * gain_ref[...]


def joined_rows(first, received, hidden, ids, route, inputs, gain):
    return pl.pallas_call(
        join,
        out_shape=jax.ShapeDtypeStruct(inputs.shape, F32),
        in_specs=[SMEM] + [VMEM] * 6,
        out_specs=VMEM,
        compiler_params=pltpu.CompilerParams(vmem_limit_bytes=24 << 20),
    )(first, in_vmem(received), hidden, ids, route, inputs, gain.reshape(1, -1))


def on_device(
    inputs,
    norm_gain,
    dense_gate,
    dense_up,
    dense_down,
    expert_gate,
    expert_up,
    expert_down,
    expert_ids,
    route_weights,
    out_gain,
):
    rows_own = inputs.shape[0]
    my_index = lax.axis_index("ep")
    ids, route = expert_ids.T, route_weights.T
    hidden_in = normed(inputs, norm_gain, expert_gate.nbytes + expert_down.nbytes)
    gathered, places = gathered_rows(hidden_in, "ep")
    partial = branch_sums(
        my_index[None],
        gathered,
        places,
        ids,
        route,
        expert_gate,
        expert_up,
        dense_gate,
        dense_up,
        dense_down,
        expert_down,
    )
    received = lax.all_to_all(partial, "ep", 0, 0, tiled=True)
    return joined_rows(
        (my_index * rows_own)[None], received, hidden_in, ids, route, inputs, out_gain
    )


def solution(mesh):
    placed = (
        P(("groups", "ep"), None),
        P(),
        P(None, "ep"),
        P(None, "ep"),
        P("ep", None),
        P(None, "ep"),
        P(None, "ep"),
        P("ep", None),
        P("groups", None),
        P("groups", None),
        P(),
    )
    return jax.shard_map(
        on_device, mesh=mesh, in_specs=placed, out_specs=P(("groups", "ep"), None), check_vma=False
    )
```

```python
import functools

import jax
import jax.numpy as jnp
from jax import lax
from jax.experimental import pallas as pl
from jax.experimental.pallas import tpu as pltpu
from jax.sharding import PartitionSpec as P

EXPERTS = 16
FLOPS_PER_BYTE = 1000
VMEM_GRANT = 14 << 20
BF16, F32 = jnp.bfloat16, jnp.float32
VMEM = pl.BlockSpec(memory_space=pltpu.VMEM)
SMEM = pl.BlockSpec(memory_space=pltpu.SMEM)
HBM = pl.BlockSpec(memory_space=pl.ANY)


def in_hbm(array):
    return pltpu.with_memory_space_constraint(array, pltpu.HBM)


def in_vmem(array):
    return pltpu.with_memory_space_constraint(array, pltpu.VMEM)


def block_of(extent, most):
    fits = [b for b in range(128, min(most, extent) + 1, 128) if extent % b == 0]
    return fits[-1] if fits else extent


def rms_scale(values):
    return values * lax.rsqrt(jnp.mean(values * values, axis=-1, keepdims=True) + 1e-06)


def norm_rows(inputs_ref, gain_ref, out_ref):
    out_ref[...] = (rms_scale(inputs_ref[...]) * gain_ref[...]).astype(out_ref.dtype)


def normed(inputs, gain, ahead):
    return pl.pallas_call(
        norm_rows,
        out_shape=jax.ShapeDtypeStruct(inputs.shape, BF16),
        in_specs=[VMEM, VMEM],
        out_specs=VMEM,
        compiler_params=pltpu.CompilerParams(vmem_limit_bytes=1 << 20),
        cost_estimate=pl.CostEstimate(
            flops=FLOPS_PER_BYTE * ahead, bytes_accessed=inputs.nbytes, transcendentals=0
        ),
    )(in_hbm(inputs), in_hbm(gain.reshape(1, -1)))


def gathered_rows(own, axis):
    devices = lax.axis_size(axis)
    assert devices & (devices - 1) == 0
    rows, places = own[None], [0]
    stages = [[1 << b] for b in range(2, devices.bit_length() - 1)] + [[1, 2]]
    for bits in stages:
        among = [0]
        for bit in bits:
            among = among + [k | bit for k in among]
        groups = [[i | k for k in among] for i in range(devices) if not i & among[-1]]
        rows = lax.all_gather(rows, axis, axis=0, tiled=True, axis_index_groups=groups)
        places = [p | k for k in among for p in places]
    return rows, places


def aligned(step, size):
    return pl.ds(pl.multiple_of(step * size, size), size)


def column_weights(expert, places, ids_ref, route_ref):
    count = ids_ref.shape[1]
    rows = count // len(places)
    across = jnp.sum(
        jnp.where(ids_ref[...] == expert, route_ref[...].astype(F32) / 1024.0, 0.0),
        axis=0,
        keepdims=True,
    )
    at = lax.broadcasted_iota(jnp.int32, (count, 1), 0)
    row = jnp.zeros_like(at)
    for k, place in enumerate(places):
        shift = (place - k) * rows
        row = jnp.where((at >= k * rows) & (at < (k + 1) * rows), at + shift, row)
    same = row == lax.broadcasted_iota(jnp.int32, (count, count), 1)
    return jnp.sum(jnp.where(same, across, 0.0), axis=1, keepdims=True)


def branches(
    places,
    slices,
    me_ref,
    rows_ref,
    ids_ref,
    route_ref,
    eg_ref,
    eu_ref,
    dg_ref,
    du_ref,
    dd_ref,
    ed_ref,
    out_ref,
    slots,
    halves,
    rows_flat,
    eg_sum,
    eu_sum,
    dg_sum,
    du_sum,
    e_hidden,
    d_hidden,
    routed,
    sems,
):
    count, width = rows_flat.shape
    rows = count // len(places)
    depth, high, units = slots.shape
    dense = dg_ref.shape[1]
    steps, parts = width // high, -(-dense // high)
    tall, blocks = dense // parts, width // units
    ends = (steps, 2 * steps, 2 * steps + parts * blocks)

    def half(k, slot):
        if dense % 128:
            return halves.at[k, slot]
        return slots.at[slot, :, pl.ds(k * dense, dense)]

    def pair(ref, at, buffer, sem):
        return pltpu.make_async_copy(ref.at[at], buffer, sem)

    def up_copies(item, slot):
        return [pair(eu_ref, (aligned(item, high), slice(None)), slots.at[slot], sems.at[0, slot])]

    def branch_copies(item, slot):
        at = (aligned(item - ends[0], high), slice(None))
        return [
            pair(ref, at, half(k, slot), sems.at[k, slot]) for k, ref in enumerate((dg_ref, du_ref))
        ]

    def last_copies(item, slot):
        item = item - ends[1]
        at = (aligned(lax.rem(item, parts), tall), aligned(lax.div(item, parts), units))
        return [pair(dd_ref, at, slots.at[slot, pl.ds(0, tall), :], sems.at[0, slot])]

    def bring(item):
        slot = lax.rem(item, depth)
        firsts = (0, *ends[:2])
        for first, end, copies in zip(firsts, ends, (up_copies, branch_copies, last_copies)):

            @pl.when((item >= first) & (item < end))
            def _():
                for copy in copies(item, slot):
                    copy.start()

    def wait(copies, item):
        slot = lax.rem(item, depth)
        for copy in copies(item, slot):
            copy.wait()
        return slot

    for item in range(depth):
        bring(jnp.int32(item))
    rows_flat[...] = rows_ref[...].reshape(count, width)
    for total in (eg_sum, eu_sum, dg_sum, du_sum):
        total[...] = jnp.zeros_like(total)

    def add(total, at, block):
        total[...] += jnp.dot(rows_flat[:, at], block[...], preferred_element_type=F32)

    widest = block_of(width, 4 * high)

    def expert_gate(step, _):
        at = aligned(step, widest)
        add(eg_sum, at, eg_ref.at[at, :])
        return 0

    def expert_up(step, _):
        slot = wait(up_copies, step)
        add(eu_sum, aligned(step, high), slots.at[slot])
        bring(step + depth)
        return 0

    lax.fori_loop(0, width // widest, expert_gate, 0)
    lax.fori_loop(0, steps, expert_up, 0)
    e_hidden[...] = (jax.nn.silu(eg_sum[...]) * eu_sum[...]).astype(BF16)
    weight = column_weights(me_ref[0] // slices, places, ids_ref, route_ref)

    def expert_down(step, _):
        at, item = aligned(step, high), step + ends[0]
        slot = wait(branch_copies, item)
        add(dg_sum, at, half(0, slot))
        add(du_sum, at, half(1, slot))
        routed[:, at] = weight * jnp.dot(
            e_hidden[...], ed_ref[:, at], preferred_element_type=F32
        )
        bring(item + depth)
        return 0

    lax.fori_loop(0, steps, expert_down, 0)
    d_hidden[...] = (jax.nn.silu(dg_sum[...]) * du_sum[...]).astype(BF16)

    def dense_down(step, _):
        at, item = aligned(step, units), step * parts + ends[1]
        part = routed[:, at]
        for k in range(parts):
            slot = wait(last_copies, item + k)
            part += jnp.dot(
                d_hidden[:, k * tall : (k + 1) * tall],
                slots[slot, :tall, :],
                preferred_element_type=F32,
            )
            bring(item + k + depth)
        part = part.astype(out_ref.dtype).reshape(len(places), rows, units)
        for k, place in enumerate(places):
            out_ref[place, :, at] = part[k]
        return 0

    lax.fori_loop(0, blocks, dense_down, 0)


def branch_sums(me, gathered, places, ids, route, e_gate, e_up, d_gate, d_up, d_down, e_down):
    devices, rows, width = gathered.shape
    count = devices * rows
    dense, units = d_gate.shape[1], e_gate.shape[1]
    high, depth = block_of(width, 512), 5
    assert width % units == 0 and dense % -(-dense // high) == 0
    assert dense % 128 or 2 * dense <= units
    halves = (2, depth, high, dense) if dense % 128 else (2, 1, 16, 128)
    weights = [
        in_vmem(e_gate),
        in_hbm(e_up),
        in_hbm(d_gate),
        in_hbm(d_up),
        in_hbm(d_down),
        in_vmem(e_down),
    ]
    return pl.pallas_call(
        functools.partial(branches, places, devices // EXPERTS),
        out_shape=jax.ShapeDtypeStruct((devices, rows, width), BF16),
        in_specs=[SMEM] + [VMEM] * 4 + [HBM] * 4 + [VMEM],
        out_specs=VMEM,
        scratch_shapes=[
            pltpu.VMEM((depth, high, units), BF16),
            pltpu.VMEM(halves, BF16),
            pltpu.VMEM((count, width), BF16),
            pltpu.VMEM((count, units), F32),
            pltpu.VMEM((count, units), F32),
            pltpu.VMEM((count, dense), F32),
            pltpu.VMEM((count, dense), F32),
            pltpu.VMEM((count, units), BF16),
            pltpu.VMEM((count, dense), BF16),
            pltpu.VMEM((count, width), F32),
            pltpu.SemaphoreType.DMA((2, depth)),
        ],
        compiler_params=pltpu.CompilerParams(vmem_limit_bytes=VMEM_GRANT),
        cost_estimate=pl.CostEstimate(
            flops=6 * count * width * (dense + units),
            bytes_accessed=6 * width * (dense + units),
            transcendentals=count * (dense + units),
        ),
    )(me, in_vmem(gathered), ids, route, *weights)


def join(
    first_ref, received_ref, hidden_ref, ids_ref, route_ref, inputs_ref, gain_ref, out_ref
):
    rows = inputs_ref.shape[0]
    summed = jnp.sum(received_ref[...].astype(F32), axis=0)
    count = ids_ref.shape[1]
    across = jnp.sum(
        jnp.where(ids_ref[...] == EXPERTS, route_ref[...].astype(F32) / 1024.0, 0.0),
        axis=0,
        keepdims=True,
    )
    mine = lax.broadcasted_iota(jnp.int32, (rows, count), 1) == first_ref[
        0
    ] + lax.broadcasted_iota(jnp.int32, (rows, count), 0)
    zero_weight = jnp.sum(jnp.where(mine, across, 0.0), axis=1, keepdims=True)
    joined = summed + zero_weight * hidden_ref[...].astype(F32)
    out_ref[...] = inputs_ref[...] + rms_scale(joined) * gain_ref[...]


def joined_rows(first, received, hidden, ids, route, inputs, gain):
    return pl.pallas_call(
        join,
        out_shape=jax.ShapeDtypeStruct(inputs.shape, F32),
        in_specs=[SMEM] + [VMEM] * 6,
        out_specs=VMEM,
        compiler_params=pltpu.CompilerParams(vmem_limit_bytes=24 << 20),
    )(first, in_vmem(received), hidden, ids, route, inputs, gain.reshape(1, -1))


def on_device(
    inputs,
    norm_gain,
    dense_gate,
    dense_up,
    dense_down,
    expert_gate,
    expert_up,
    expert_down,
    expert_ids,
    route_weights,
    out_gain,
):
    rows_own = inputs.shape[0]
    my_index = lax.axis_index("ep")
    ids, route = expert_ids.T, route_weights.T
    hidden_in = normed(inputs, norm_gain, expert_gate.nbytes + expert_down.nbytes)
    gathered, places = gathered_rows(hidden_in, "ep")
    partial = branch_sums(
        my_index[None],
        gathered,
        places,
        ids,
        route,
        expert_gate,
        expert_up,
        dense_gate,
        dense_up,
        dense_down,
        expert_down,
    )
    received = lax.all_to_all(partial, "ep", 0, 0, tiled=True)
    return joined_rows(
        (my_index * rows_own)[None], received, hidden_in, ids, route, inputs, out_gain
    )


def solution(mesh):
    placed = (
        P(("groups", "ep"), None),
        P(),
        P(None, "ep"),
        P(None, "ep"),
        P("ep", None),
        P(None, "ep"),
        P(None, "ep"),
        P("ep", None),
        P("groups", None),
        P("groups", None),
        P(),
    )
    return jax.shard_map(
        on_device, mesh=mesh, in_specs=placed, out_specs=P(("groups", "ep"), None), check_vma=False
    )
```

```python
import functools

import jax
import jax.numpy as jnp
from jax import lax
from jax.experimental import pallas as pl
from jax.experimental.pallas import tpu as pltpu
from jax.sharding import PartitionSpec as P

EXPERTS = 16
FLOPS_PER_BYTE = 1000
TILE = 256
VMEM_GRANT = 15 << 20
BF16, F32 = jnp.bfloat16, jnp.float32
VMEM = pl.BlockSpec(memory_space=pltpu.VMEM)
SMEM = pl.BlockSpec(memory_space=pltpu.SMEM)
HBM = pl.BlockSpec(memory_space=pl.ANY)


def in_hbm(array):
    return pltpu.with_memory_space_constraint(array, pltpu.HBM)


def in_vmem(array):
    return pltpu.with_memory_space_constraint(array, pltpu.VMEM)


def block_of(extent, most):
    fits = [b for b in range(128, min(most, extent) + 1, 128) if extent % b == 0]
    return fits[-1] if fits else extent


def rms_scale(values):
    return values * lax.rsqrt(jnp.mean(values * values, axis=-1, keepdims=True) + 1e-06)


def norm_rows(inputs_ref, gain_ref, out_ref):
    out_ref[...] = (rms_scale(inputs_ref[...]) * gain_ref[...]).astype(out_ref.dtype)


def normed(inputs, gain, ahead):
    return pl.pallas_call(
        norm_rows,
        out_shape=jax.ShapeDtypeStruct(inputs.shape, BF16),
        in_specs=[VMEM, VMEM],
        out_specs=VMEM,
        compiler_params=pltpu.CompilerParams(vmem_limit_bytes=1 << 20),
        cost_estimate=pl.CostEstimate(
            flops=FLOPS_PER_BYTE * ahead, bytes_accessed=inputs.nbytes, transcendentals=0
        ),
    )(in_hbm(inputs), in_hbm(gain.reshape(1, -1)))


def gathered_rows(own, axis):
    devices = lax.axis_size(axis)
    assert devices & (devices - 1) == 0
    rows, places = own[None], [0]
    stages = [[1 << b] for b in range(2, devices.bit_length() - 1)] + [[1, 2]]
    for bits in stages:
        among = [0]
        for bit in bits:
            among = among + [k | bit for k in among]
        groups = [[i | k for k in among] for i in range(devices) if not i & among[-1]]
        rows = lax.all_gather(rows, axis, axis=0, tiled=True, axis_index_groups=groups)
        places = [p | k for k in among for p in places]
    return rows, places


def aligned(step, size):
    return pl.ds(pl.multiple_of(step * size, size), size)


def column_weights(expert, places, ids_ref, route_ref):
    count = ids_ref.shape[1]
    rows = count // len(places)
    across = jnp.sum(
        jnp.where(ids_ref[...] == expert, route_ref[...].astype(F32) / 1024.0, 0.0),
        axis=0,
        keepdims=True,
    )
    at = lax.broadcasted_iota(jnp.int32, (count, 1), 0)
    row = jnp.zeros_like(at)
    for k, place in enumerate(places):
        shift = (place - k) * rows
        row = jnp.where((at >= k * rows) & (at < (k + 1) * rows), at + shift, row)
    same = row == lax.broadcasted_iota(jnp.int32, (count, count), 1)
    return jnp.sum(jnp.where(same, across, 0.0), axis=1, keepdims=True)


def accumulators(rows, count):
    return [pltpu.ACC(j % 2)((rows, TILE), F32) for j in range(count)]


def multiply(turns, sums, lefts, right):
    for k, left in enumerate(lefts):
        for j, total in enumerate(sums):
            unit = j % 2
            stage = turns[unit] % 2
            turns[unit] += 1
            pltpu.matmul_push_rhs(right(k, j), stage, unit)
            pltpu.matmul_acc_lhs(total, left, load_staged_rhs=stage)


def tile_products(sizes, calls, refs, eg_acc, eu_acc, d_acc, routed_acc, last_acc):
    steps, parts, blocks, ends, depth, tall = sizes
    wait, bring, up_copies, branch_copies, last_copies, half, weights, write, flatten = calls
    eg_ref, ed_ref, slots, rows_flat, e_hidden, d_hidden, routed = refs
    _, high, units = slots.shape
    deep, thin = high // TILE, len(d_acc) // 2

    def tile(k):
        return pl.ds(k * TILE, TILE)

    def row_tiles(step):
        return [rows_flat[:, aligned(step * deep + k, TILE)] for k in range(deep)]

    def expert_gate(step, _):
        def right(k, j):
            return eg_ref[aligned(step * deep + k, TILE), tile(j)]

        flatten(aligned(step, high), high)
        multiply([0, 0], eg_acc, row_tiles(step), right)
        return 0

    def expert_up(step, _):
        slot = wait(up_copies, step)
        multiply([0, 0], eu_acc, row_tiles(step), lambda k, j: slots[slot, tile(k), tile(j)])
        bring(step + depth)
        return 0

    lax.fori_loop(0, steps, expert_gate, 0)
    lax.fori_loop(0, steps, expert_up, 0)
    for j, (gate, upper) in enumerate(zip(eg_acc, eu_acc)):
        hidden = jax.nn.silu(pltpu.matmul_pop(gate)) * pltpu.matmul_pop(upper)
        e_hidden[:, j * TILE : (j + 1) * TILE] = hidden.astype(BF16)
    weight = weights()

    def expert_down(step, _):
        item, turns = step + ends[0], [0, 0]

        def right(k, j):
            return ed_ref[tile(k), aligned(step * deep + j, TILE)]

        lefts = [e_hidden[:, k * TILE : (k + 1) * TILE] for k in range(units // TILE)]
        multiply(turns, routed_acc, lefts, right)
        slot = wait(branch_copies, item)
        gate, upper = half(0, slot), half(1, slot)

        def dense_right(k, j):
            return (gate if j < thin else upper)[tile(k), tile(j % thin)]

        multiply(turns, d_acc, row_tiles(step), dense_right)
        for j, total in enumerate(routed_acc):
            routed[:, aligned(step * deep + j, TILE)] = weight * pltpu.matmul_pop(total)
        bring(item + depth)
        return 0

    lax.fori_loop(0, steps, expert_down, 0)
    for j in range(thin):
        hidden = jax.nn.silu(pltpu.matmul_pop(d_acc[j])) * pltpu.matmul_pop(d_acc[thin + j])
        d_hidden[:, j * TILE : (j + 1) * TILE] = hidden.astype(BF16)

    def dense_down(step, _):
        item, turns = step * parts + ends[1], [0, 0]
        for k in range(parts):
            slot = wait(last_copies, item + k)
            left = d_hidden[:, k * TILE : (k + 1) * TILE]
            multiply(turns, last_acc, [left], lambda _, j: slots[slot, pl.ds(0, TILE), tile(j)])
            bring(item + k + depth)
        for j, total in enumerate(last_acc):
            at = aligned(step * len(last_acc) + j, TILE)
            write(at, pltpu.matmul_pop(total) + routed[:, at])
        return 0

    lax.fori_loop(0, blocks, dense_down, 0)


def branches(
    places,
    slices,
    me_ref,
    rows_ref,
    ids_ref,
    route_ref,
    eg_ref,
    eu_ref,
    dg_ref,
    du_ref,
    dd_ref,
    ed_ref,
    out_ref,
    slots,
    halves,
    rows_flat,
    eg_sum,
    eu_sum,
    dg_sum,
    du_sum,
    e_hidden,
    d_hidden,
    routed,
    ids_here,
    route_here,
    sems,
    route_sems,
    *,
    explicit,
):
    count, width = rows_flat.shape
    rows = count // len(places)
    depth, high, units = slots.shape
    dense = dg_ref.shape[1]
    steps, parts = width // high, dense // TILE if explicit else -(-dense // high)
    tall, blocks = dense // parts, width // units
    ends = (steps, 2 * steps, 2 * steps + parts * blocks)

    def half(k, slot):
        if dense % 128:
            return halves.at[k, slot]
        return slots.at[slot, :, pl.ds(k * dense, dense)]

    def pair(ref, at, buffer, sem):
        return pltpu.make_async_copy(ref.at[at], buffer, sem)

    def up_copies(item, slot):
        return [pair(eu_ref, (aligned(item, high), slice(None)), slots.at[slot], sems.at[0, slot])]

    def branch_copies(item, slot):
        at = (aligned(item - ends[0], high), slice(None))
        return [
            pair(ref, at, half(k, slot), sems.at[k, slot]) for k, ref in enumerate((dg_ref, du_ref))
        ]

    def last_copies(item, slot):
        item = item - ends[1]
        at = (aligned(lax.rem(item, parts), tall), aligned(lax.div(item, parts), units))
        return [pair(dd_ref, at, slots.at[slot, pl.ds(0, tall), :], sems.at[0, slot])]

    def bring(item):
        slot = lax.rem(item, depth)
        firsts = (0, *ends[:2])
        for first, end, copies in zip(firsts, ends, (up_copies, branch_copies, last_copies)):

            @pl.when((item >= first) & (item < end))
            def _():
                for copy in copies(item, slot):
                    copy.start()

    def wait(copies, item):
        slot = lax.rem(item, depth)
        for copy in copies(item, slot):
            copy.wait()
        return slot

    for item in range(depth):
        bring(jnp.int32(item))
    route_copies = [
        pltpu.make_async_copy(ids_ref, ids_here, route_sems.at[0]),
        pltpu.make_async_copy(route_ref, route_here, route_sems.at[1]),
    ]
    for copy in route_copies:
        copy.start()

    def flatten(at, wide):
        rows_flat[:, at] = rows_ref[:, :, at].reshape(count, wide)
    def weights():
        for copy in route_copies:
            copy.wait()
        return column_weights(me_ref[0] // slices, places, ids_here, route_here)

    def write(at, part):
        part = part.astype(out_ref.dtype).reshape(len(places), rows, part.shape[1])
        for k, place in enumerate(places):
            out_ref[place, :, at] = part[k]

    on_tiles = functools.partial(
        tile_products,
        (steps, parts, blocks, ends, depth, tall),
        (wait, bring, up_copies, branch_copies, last_copies, half, weights, write, flatten),
        (eg_ref, ed_ref, slots, rows_flat, e_hidden, d_hidden, routed),
    )
    if explicit:
        wide, thin = units // TILE, dense // TILE
        pl.run_scoped(
            on_tiles, *[accumulators(count, n) for n in (wide, wide, 2 * thin, high // TILE, wide)]
        )
        return
    flatten(slice(None), width)
    for total in (eg_sum, eu_sum, dg_sum, du_sum):
        total[...] = jnp.zeros_like(total)

    def add(total, at, block):
        total[...] += jnp.dot(rows_flat[:, at], block[...], preferred_element_type=F32)

    widest = block_of(width, 4 * high)

    def expert_gate(step, _):
        at = aligned(step, widest)
        add(eg_sum, at, eg_ref.at[at, :])
        return 0

    def expert_up(step, _):
        slot = wait(up_copies, step)
        add(eu_sum, aligned(step, high), slots.at[slot])
        bring(step + depth)
        return 0

    lax.fori_loop(0, width // widest, expert_gate, 0)
    lax.fori_loop(0, steps, expert_up, 0)
    e_hidden[...] = (jax.nn.silu(eg_sum[...]) * eu_sum[...]).astype(BF16)
    weight = weights()

    def expert_down(step, _):
        at, item = aligned(step, high), step + ends[0]
        slot = wait(branch_copies, item)
        add(dg_sum, at, half(0, slot))
        add(du_sum, at, half(1, slot))
        routed[:, at] = weight * jnp.dot(
            e_hidden[...], ed_ref[:, at], preferred_element_type=F32
        )
        bring(item + depth)
        return 0

    lax.fori_loop(0, steps, expert_down, 0)
    d_hidden[...] = (jax.nn.silu(dg_sum[...]) * du_sum[...]).astype(BF16)

    def dense_down(step, _):
        at, item = aligned(step, units), step * parts + ends[1]
        part = routed[:, at]
        for k in range(parts):
            slot = wait(last_copies, item + k)
            part += jnp.dot(
                d_hidden[:, k * tall : (k + 1) * tall],
                slots[slot, :tall, :],
                preferred_element_type=F32,
            )
            bring(item + k + depth)
        write(at, part)
        return 0

    lax.fori_loop(0, blocks, dense_down, 0)


def branch_sums(me, gathered, places, ids, route, e_gate, e_up, d_gate, d_up, d_down, e_down):
    devices, rows, width = gathered.shape
    count = devices * rows
    dense, units = d_gate.shape[1], e_gate.shape[1]
    high, depth = block_of(width, 512), 6
    assert width % units == 0 and dense % -(-dense // high) == 0
    assert dense % 128 or 2 * dense <= units
    explicit = dense % TILE == 0 and units % TILE == 0 and high % TILE == 0 and count <= 64
    sums = (units, units, dense, dense)
    halves = (2, depth, high, dense) if dense % 128 else (2, 1, 16, 128)
    weights = [
        in_vmem(e_gate),
        in_hbm(e_up),
        in_hbm(d_gate),
        in_hbm(d_up),
        in_hbm(d_down),
        in_vmem(e_down),
    ]
    return pl.pallas_call(
        functools.partial(branches, places, devices // EXPERTS, explicit=explicit),
        out_shape=jax.ShapeDtypeStruct((devices, rows, width), BF16),
        in_specs=[SMEM, VMEM, HBM, HBM, VMEM, HBM, HBM, HBM, HBM, VMEM],
        out_specs=VMEM,
        scratch_shapes=[
            pltpu.VMEM((depth, high, units), BF16),
            pltpu.VMEM(halves, BF16),
            pltpu.VMEM((count, width), BF16),
            *(pltpu.VMEM((8, 128) if explicit else (count, n), F32) for n in sums),
            pltpu.VMEM((count, units), BF16),
            pltpu.VMEM((count, dense), BF16),
            pltpu.VMEM((count, width), F32),
            pltpu.VMEM(ids.shape, ids.dtype),
            pltpu.VMEM(route.shape, route.dtype),
            pltpu.SemaphoreType.DMA((2, depth)),
            pltpu.SemaphoreType.DMA((2,)),
        ],
        compiler_params=pltpu.CompilerParams(vmem_limit_bytes=VMEM_GRANT),
        cost_estimate=pl.CostEstimate(
            flops=6 * count * width * (dense + units),
            bytes_accessed=6 * width * (dense + units),
            transcendentals=count * (dense + units),
        ),
    )(me, in_vmem(gathered), in_hbm(ids), in_hbm(route), *weights)


def join(
    first_ref, received_ref, hidden_ref, ids_ref, route_ref, inputs_ref, gain_ref, out_ref
):
    rows = inputs_ref.shape[0]
    summed = jnp.sum(received_ref[...].astype(F32), axis=0)
    count = ids_ref.shape[1]
    across = jnp.sum(
        jnp.where(ids_ref[...] == EXPERTS, route_ref[...].astype(F32) / 1024.0, 0.0),
        axis=0,
        keepdims=True,
    )
    mine = lax.broadcasted_iota(jnp.int32, (rows, count), 1) == first_ref[
        0
    ] + lax.broadcasted_iota(jnp.int32, (rows, count), 0)
    zero_weight = jnp.sum(jnp.where(mine, across, 0.0), axis=1, keepdims=True)
    joined = summed + zero_weight * hidden_ref[...].astype(F32)
    out_ref[...] = inputs_ref[...] + rms_scale(joined) * gain_ref[...]


def joined_rows(first, received, hidden, ids, route, inputs, gain):
    return pl.pallas_call(
        join,
        out_shape=jax.ShapeDtypeStruct(inputs.shape, F32),
        in_specs=[SMEM] + [VMEM] * 6,
        out_specs=VMEM,
        compiler_params=pltpu.CompilerParams(vmem_limit_bytes=24 << 20),
    )(first, in_vmem(received), hidden, ids, route, inputs, gain.reshape(1, -1))


def on_device(
    inputs,
    norm_gain,
    dense_gate,
    dense_up,
    dense_down,
    expert_gate,
    expert_up,
    expert_down,
    expert_ids,
    route_weights,
    out_gain,
):
    rows_own = inputs.shape[0]
    my_index = lax.axis_index("ep")
    ids, route = expert_ids.T, route_weights.T
    hidden_in = normed(inputs, norm_gain, expert_gate.nbytes + expert_down.nbytes)
    gathered, places = gathered_rows(hidden_in, "ep")
    partial = branch_sums(
        my_index[None],
        gathered,
        places,
        ids,
        route,
        expert_gate,
        expert_up,
        dense_gate,
        dense_up,
        dense_down,
        expert_down,
    )
    received = lax.all_to_all(partial, "ep", 0, 0, tiled=True)
    return joined_rows(
        (my_index * rows_own)[None], received, hidden_in, ids, route, inputs, out_gain
    )


def solution(mesh):
    placed = (
        P(("groups", "ep"), None),
        P(),
        P(None, "ep"),
        P(None, "ep"),
        P("ep", None),
        P(None, "ep"),
        P(None, "ep"),
        P("ep", None),
        P("groups", None),
        P("groups", None),
        P(),
    )
    def program(*args):
        with jax.sharding.use_abstract_mesh(mesh.abstract_mesh):
            return sharded(*args)

    sharded = jax.shard_map(
        on_device, mesh=mesh, in_specs=placed, out_specs=P(("groups", "ep"), None), check_vma=False
    )
    return program
```

```python
import functools

import jax
import jax.numpy as jnp
from jax import lax
from jax.experimental import pallas as pl
from jax.experimental.pallas import tpu as pltpu
from jax.sharding import PartitionSpec as P

EXPERTS = 16
FLOPS_PER_BYTE = 1000
TILE = 256
VMEM_GRANT = 15 << 20
BF16, F32 = jnp.bfloat16, jnp.float32
VMEM = pl.BlockSpec(memory_space=pltpu.VMEM)
HBM = pl.BlockSpec(memory_space=pl.ANY)


def in_hbm(array):
    return pltpu.with_memory_space_constraint(array, pltpu.HBM)


def in_vmem(array):
    return pltpu.with_memory_space_constraint(array, pltpu.VMEM)


def block_of(extent, most):
    fits = [b for b in range(128, min(most, extent) + 1, 128) if extent % b == 0]
    return fits[-1] if fits else extent


def rms_scale(values):
    return values * lax.rsqrt(jnp.mean(values * values, axis=-1, keepdims=True) + 1e-06)


def norm_rows(inputs_ref, gain_ref, out_ref):
    out_ref[...] = (rms_scale(inputs_ref[...]) * gain_ref[...]).astype(out_ref.dtype)


def normed(inputs, gain, ahead):
    return pl.pallas_call(
        norm_rows,
        out_shape=jax.ShapeDtypeStruct(inputs.shape, BF16),
        in_specs=[VMEM, VMEM],
        out_specs=VMEM,
        compiler_params=pltpu.CompilerParams(vmem_limit_bytes=1 << 20),
        cost_estimate=pl.CostEstimate(
            flops=FLOPS_PER_BYTE * ahead, bytes_accessed=inputs.nbytes, transcendentals=0
        ),
    )(in_hbm(inputs), in_hbm(gain.reshape(1, -1)))


def gathered_rows(own, axis):
    devices = lax.axis_size(axis)
    assert devices & (devices - 1) == 0
    rows, places = own[None], [0]
    stages = [[1 << b] for b in range(2, devices.bit_length() - 1)] + [[1, 2]]
    for bits in stages:
        among = [0]
        for bit in bits:
            among = among + [k | bit for k in among]
        groups = [[i | k for k in among] for i in range(devices) if not i & among[-1]]
        rows = lax.all_gather(rows, axis, axis=0, tiled=True, axis_index_groups=groups)
        places = [p | k for k in among for p in places]
    return rows, places


def aligned(step, size):
    return pl.ds(pl.multiple_of(step * size, size), size)


def column_weights(expert, places, ids_ref, route_ref):
    count = ids_ref.shape[1]
    rows = count // len(places)
    across = jnp.sum(
        jnp.where(ids_ref[...] == expert, route_ref[...].astype(F32) / 1024.0, 0.0),
        axis=0,
        keepdims=True,
    )
    at = lax.broadcasted_iota(jnp.int32, (count, 1), 0)
    row = jnp.zeros_like(at)
    for k, place in enumerate(places):
        shift = (place - k) * rows
        row = jnp.where((at >= k * rows) & (at < (k + 1) * rows), at + shift, row)
    same = row == lax.broadcasted_iota(jnp.int32, (count, count), 1)
    return jnp.sum(jnp.where(same, across, 0.0), axis=1, keepdims=True)


def accumulators(rows, count):
    return [pltpu.ACC(j % 2)((rows, TILE), F32) for j in range(count)]


def multiply(turns, sums, lefts, right):
    for k, left in enumerate(lefts):
        for j, total in enumerate(sums):
            unit = j % 2
            stage = turns[unit] % 2
            turns[unit] += 1
            pltpu.matmul_push_rhs(right(k, j), stage, unit)
            pltpu.matmul_acc_lhs(total, left, load_staged_rhs=stage)


def tile_products(sizes, calls, refs, eg_acc, eu_acc, d_acc, routed_acc, last_acc):
    steps, parts, blocks, ends, depth, tall = sizes
    wait, bring, up_copies, branch_copies, last_copies, half, weights, write, rows_at, before, out_copy = calls
    eg_ref, ed_ref, slots, e_hidden, d_hidden, routed = refs
    _, high, units = slots.shape
    deep, thin = high // TILE, len(d_acc) // 2

    def tile(k):
        return pl.ds(k * TILE, TILE)

    def row_tiles(step):
        return [rows_at(aligned(step * deep + k, TILE), TILE) for k in range(deep)]

    def expert_gate(step, _):
        def right(k, j):
            return eg_ref[aligned(step * deep + k, TILE), tile(j)]

        multiply([0, 0], eg_acc, row_tiles(step), right)
        return 0

    def expert_up(step, _):
        slot = wait(up_copies, step)
        multiply([0, 0], eu_acc, row_tiles(step), lambda k, j: slots[slot, tile(k), tile(j)])
        bring(step + depth)
        return 0

    lax.fori_loop(0, steps, expert_gate, 0, unroll=3)
    lax.fori_loop(0, steps, expert_up, 0)
    for j, (gate, upper) in enumerate(zip(eg_acc, eu_acc)):
        hidden = jax.nn.silu(pltpu.matmul_pop(gate)) * pltpu.matmul_pop(upper)
        e_hidden[:, j * TILE : (j + 1) * TILE] = hidden.astype(BF16)
    weight = weights()

    def expert_down(step, _):
        item, turns = step + ends[0], [0, 0]

        def right(k, j):
            return ed_ref[tile(k), aligned(step * deep + j, TILE)]

        lefts = [e_hidden[:, k * TILE : (k + 1) * TILE] for k in range(units // TILE)]
        multiply(turns, routed_acc, lefts, right)
        slot = wait(branch_copies, item)
        gate, upper = half(0, slot), half(1, slot)

        def dense_right(k, j):
            return (gate if j < thin else upper)[tile(k), tile(j % thin)]

        multiply(turns, d_acc, row_tiles(step), dense_right)
        for j, total in enumerate(routed_acc):
            routed[:, aligned(step * deep + j, TILE)] = weight * pltpu.matmul_pop(total)
        bring(item + depth)
        return 0

    lax.fori_loop(0, steps, expert_down, 0)
    for j in range(thin):
        hidden = jax.nn.silu(pltpu.matmul_pop(d_acc[j])) * pltpu.matmul_pop(d_acc[thin + j])
        d_hidden[:, j * TILE : (j + 1) * TILE] = hidden.astype(BF16)

    def dense_down(step, _):
        item, turns = step * parts + ends[1], [0, 0]
        for k in range(parts):
            slot = wait(last_copies, item + k)
            left = d_hidden[:, k * TILE : (k + 1) * TILE]
            multiply(turns, last_acc, [left], lambda _, j: slots[slot, pl.ds(0, TILE), tile(j)])
            bring(item + k + depth)
        here = before(step)
        for j, total in enumerate(last_acc):
            at = aligned(step * len(last_acc) + j, TILE)
            write(here, tile(j), pltpu.matmul_pop(total) + routed[:, at])
        out_copy(step).start()
        return 0

    lax.fori_loop(0, blocks, dense_down, 0)


def branches(
    places,
    slices,
    rows_ref,
    ids_ref,
    route_ref,
    eg_ref,
    eu_ref,
    dg_ref,
    du_ref,
    dd_ref,
    ed_ref,
    out_ref,
    slots,
    halves,
    rows_flat,
    eg_sum,
    eu_sum,
    dg_sum,
    du_sum,
    e_hidden,
    d_hidden,
    routed,
    ids_here,
    route_here,
    out_here,
    sems,
    route_sems,
    out_sems,
    *,
    explicit,
):
    _, rows, width = rows_ref.shape
    count = rows * len(places)
    depth, high, units = slots.shape
    dense = dg_ref.shape[1]
    steps, parts = width // high, dense // TILE if explicit else -(-dense // high)
    tall, blocks = dense // parts, width // units
    ends = (steps, 2 * steps, 2 * steps + parts * blocks)

    def half(k, slot):
        if dense % 128:
            return halves.at[k, slot]
        return slots.at[slot, :, pl.ds(k * dense, dense)]

    def pair(ref, at, buffer, sem):
        return pltpu.make_async_copy(ref.at[at], buffer, sem)

    def up_copies(item, slot):
        return [pair(eu_ref, (aligned(item, high), slice(None)), slots.at[slot], sems.at[0, slot])]

    def branch_copies(item, slot):
        at = (aligned(item - ends[0], high), slice(None))
        return [
            pair(ref, at, half(k, slot), sems.at[k, slot]) for k, ref in enumerate((dg_ref, du_ref))
        ]

    def last_copies(item, slot):
        item = item - ends[1]
        at = (aligned(lax.rem(item, parts), tall), aligned(lax.div(item, parts), units))
        return [pair(dd_ref, at, slots.at[slot, pl.ds(0, tall), :], sems.at[0, slot])]

    def bring(item):
        slot = lax.rem(item, depth)
        firsts = (0, *ends[:2])
        for first, end, copies in zip(firsts, ends, (up_copies, branch_copies, last_copies)):

            @pl.when((item >= first) & (item < end))
            def _():
                for copy in copies(item, slot):
                    copy.start()

    def wait(copies, item):
        slot = lax.rem(item, depth)
        for copy in copies(item, slot):
            copy.wait()
        return slot

    for item in range(depth):
        bring(jnp.int32(item))
    route_copies = [
        pltpu.make_async_copy(ids_ref, ids_here, route_sems.at[0]),
        pltpu.make_async_copy(route_ref, route_here, route_sems.at[1]),
    ]
    for copy in route_copies:
        copy.start()

    def rows_at(at, wide):
        return rows_ref[:, :, at].reshape(count, wide)
    def weights():
        for copy in route_copies:
            copy.wait()
        return column_weights(lax.axis_index("ep") // slices, places, ids_here, route_here)

    def out_copy(step):
        at = aligned(step, units)
        slot = lax.rem(step, 2)
        return pltpu.make_async_copy(out_here.at[slot], out_ref.at[:, :, at], out_sems.at[slot])

    def write(slot, at, part):
        part = part.astype(out_ref.dtype).reshape(len(places), rows, part.shape[1])
        for k, place in enumerate(places):
            out_here[slot, place, :, at] = part[k]

    def before(step):
        @pl.when(step >= 2)
        def _():
            out_copy(step - 2).wait()

        return lax.rem(step, 2)

    on_tiles = functools.partial(
        tile_products,
        (steps, parts, blocks, ends, depth, tall),
        (wait, bring, up_copies, branch_copies, last_copies, half, weights, write, rows_at, before, out_copy),
        (eg_ref, ed_ref, slots, e_hidden, d_hidden, routed),
    )
    def finish():
        for step in range(max(0, blocks - 2), blocks):
            out_copy(jnp.int32(step)).wait()

    if explicit:
        wide, thin = units // TILE, dense // TILE
        pl.run_scoped(
            on_tiles, *[accumulators(count, n) for n in (wide, wide, 2 * thin, high // TILE, wide)]
        )
        finish()
        return
    rows_flat[...] = rows_at(slice(None), width)
    for total in (eg_sum, eu_sum, dg_sum, du_sum):
        total[...] = jnp.zeros_like(total)

    def add(total, at, block):
        total[...] += jnp.dot(rows_flat[:, at], block[...], preferred_element_type=F32)

    widest = block_of(width, 4 * high)

    def expert_gate(step, _):
        at = aligned(step, widest)
        add(eg_sum, at, eg_ref.at[at, :])
        return 0

    def expert_up(step, _):
        slot = wait(up_copies, step)
        add(eu_sum, aligned(step, high), slots.at[slot])
        bring(step + depth)
        return 0

    lax.fori_loop(0, width // widest, expert_gate, 0)
    lax.fori_loop(0, steps, expert_up, 0)
    e_hidden[...] = (jax.nn.silu(eg_sum[...]) * eu_sum[...]).astype(BF16)
    weight = weights()

    def expert_down(step, _):
        at, item = aligned(step, high), step + ends[0]
        slot = wait(branch_copies, item)
        add(dg_sum, at, half(0, slot))
        add(du_sum, at, half(1, slot))
        routed[:, at] = weight * jnp.dot(
            e_hidden[...], ed_ref[:, at], preferred_element_type=F32
        )
        bring(item + depth)
        return 0

    lax.fori_loop(0, steps, expert_down, 0)
    d_hidden[...] = (jax.nn.silu(dg_sum[...]) * du_sum[...]).astype(BF16)

    def dense_down(step, _):
        at, item = aligned(step, units), step * parts + ends[1]
        part = routed[:, at]
        for k in range(parts):
            slot = wait(last_copies, item + k)
            part += jnp.dot(
                d_hidden[:, k * tall : (k + 1) * tall],
                slots[slot, :tall, :],
                preferred_element_type=F32,
            )
            bring(item + k + depth)
        write(before(step), slice(None), part)
        out_copy(step).start()
        return 0

    lax.fori_loop(0, blocks, dense_down, 0)
    finish()


def branch_sums(gathered, places, ids, route, e_gate, e_up, d_gate, d_up, d_down, e_down):
    devices, rows, width = gathered.shape
    count = devices * rows
    dense, units = d_gate.shape[1], e_gate.shape[1]
    high, depth = block_of(width, 512), 6
    assert width % units == 0 and dense % -(-dense // high) == 0
    assert dense % 128 or 2 * dense <= units
    explicit = dense % TILE == 0 and units % TILE == 0 and high % TILE == 0 and count <= 64
    sums = (units, units, dense, dense)
    halves = (2, depth, high, dense) if dense % 128 else (2, 1, 16, 128)
    weights = [
        in_vmem(e_gate),
        in_hbm(e_up),
        in_hbm(d_gate),
        in_hbm(d_up),
        in_hbm(d_down),
        in_vmem(e_down),
    ]
    return pl.pallas_call(
        functools.partial(branches, places, devices // EXPERTS, explicit=explicit),
        out_shape=jax.ShapeDtypeStruct((devices, rows, width), BF16),
        in_specs=[VMEM, HBM, HBM, VMEM, HBM, HBM, HBM, HBM, VMEM],
        out_specs=HBM,
        scratch_shapes=[
            pltpu.VMEM((depth, high, units), BF16),
            pltpu.VMEM(halves, BF16),
            pltpu.VMEM((16, 128) if explicit else (count, width), BF16),
            *(pltpu.VMEM((8, 128) if explicit else (count, n), F32) for n in sums),
            pltpu.VMEM((count, units), BF16),
            pltpu.VMEM((count, dense), BF16),
            pltpu.VMEM((count, width), F32),
            pltpu.VMEM(ids.shape, ids.dtype),
            pltpu.VMEM(route.shape, route.dtype),
            pltpu.VMEM((2, devices, rows, units), BF16),
            pltpu.SemaphoreType.DMA((2, depth)),
            pltpu.SemaphoreType.DMA((2,)),
            pltpu.SemaphoreType.DMA((2,)),
        ],
        compiler_params=pltpu.CompilerParams(vmem_limit_bytes=VMEM_GRANT),
        cost_estimate=pl.CostEstimate(
            flops=6 * count * width * (dense + units),
            bytes_accessed=6 * width * (dense + units),
            transcendentals=count * (dense + units),
        ),
    )(in_vmem(gathered), in_hbm(ids), in_hbm(route), *weights)


def join(
    received_ref, hidden_ref, ids_ref, route_ref, inputs_ref, gain_ref, out_ref
):
    rows = inputs_ref.shape[0]
    summed = jnp.sum(received_ref[...].astype(F32), axis=0)
    count = ids_ref.shape[1]
    across = jnp.sum(
        jnp.where(ids_ref[...] == EXPERTS, route_ref[...].astype(F32) / 1024.0, 0.0),
        axis=0,
        keepdims=True,
    )
    first = lax.axis_index("ep") * rows
    mine = lax.broadcasted_iota(jnp.int32, (rows, count), 1) == first + lax.broadcasted_iota(
        jnp.int32, (rows, count), 0
    )
    zero_weight = jnp.sum(jnp.where(mine, across, 0.0), axis=1, keepdims=True)
    joined = summed + zero_weight * hidden_ref[...].astype(F32)
    out_ref[...] = inputs_ref[...] + rms_scale(joined) * gain_ref[...]


def joined_rows(received, hidden, ids, route, inputs, gain):
    return pl.pallas_call(
        join,
        out_shape=jax.ShapeDtypeStruct(inputs.shape, F32),
        in_specs=[VMEM] * 6,
        out_specs=VMEM,
        compiler_params=pltpu.CompilerParams(vmem_limit_bytes=24 << 20),
    )(in_vmem(received), hidden, ids, route, inputs, gain.reshape(1, -1))


def on_device(
    inputs,
    norm_gain,
    dense_gate,
    dense_up,
    dense_down,
    expert_gate,
    expert_up,
    expert_down,
    expert_ids,
    route_weights,
    out_gain,
):
    ids, route = expert_ids.T, route_weights.T
    hidden_in = normed(inputs, norm_gain, expert_gate.nbytes + expert_down.nbytes)
    gathered, places = gathered_rows(hidden_in, "ep")
    partial = branch_sums(
        gathered,
        places,
        ids,
        route,
        expert_gate,
        expert_up,
        dense_gate,
        dense_up,
        dense_down,
        expert_down,
    )
    received = lax.all_to_all(partial, "ep", 0, 0, tiled=True)
    return joined_rows(
        received, hidden_in, ids, route, inputs, out_gain
    )


def solution(mesh):
    placed = (
        P(("groups", "ep"), None),
        P(),
        P(None, "ep"),
        P(None, "ep"),
        P("ep", None),
        P(None, "ep"),
        P(None, "ep"),
        P("ep", None),
        P("groups", None),
        P("groups", None),
        P(),
    )
    def program(*args):
        with jax.sharding.use_abstract_mesh(mesh.abstract_mesh):
            return sharded(*args)

    sharded = jax.shard_map(
        on_device, mesh=mesh, in_specs=placed, out_specs=P(("groups", "ep"), None), check_vma=False
    )
    return program
```
